32 devices in a mesh: band: 16 (over z, y, core), slab: 2 (over x).
Axes of the slice: x: 2, y: 2, z: 4, core: 2. Of those that a mesh axis runs over, the one named last changes fastest.
Arguments:
- orbitals: float32 [16, 160, 160, 160], P('band', 'slab'), may hold values from -6 to 6
Outputs:
- exchange_field: float32 [16, 160, 160, 160], P('band', 'slab')
The draws below stay inside these ranges and needn't reach their ends.
All inputs are finite; a program needn't handle non-finite values.
Results may differ from the reference program's by a relative error of at most 0.0003.
Values sent between devices are 32-bit elements; how exact they have to be, the bound alone decides.
A program may use at most 192 MiB of HBM per device.

```python
import math
import jax
import jax.numpy as jnp
from jax import lax

NG = 160
STEPS = 2
BANDS = 16


def draw_orbitals(key, part):
    key = jax.random.fold_in(key, 11)
    phase_key, height_key, rough_key = jax.random.split(key, 3)
    bands = jnp.arange(BANDS, dtype=jnp.int32)
    first_y = NG * 12 // 160
    first_x = NG * 3 // 160
    second_y = NG * 14 // 160
    second_x = NG * 3 // 160
    halves = bands // 2
    parity = bands % 2
    wave_y = (halves * (first_y + second_y) + parity * first_y) % NG
    wave_x = (halves * (first_x + second_x) + parity * first_x) % NG
    wave_z = bands * (NG // 4) % NG
    grid = jnp.arange(NG, dtype=jnp.int32)
    along_z = wave_z[:, None, None, None] * grid[None, :, None, None] % NG
    along_y = wave_y[:, None, None, None] * grid[None, None, :, None] % NG
    along_x = wave_x[:, None, None, None] * grid[None, None, None, :] % NG
    index = (along_z + along_y + along_x) % NG
    offsets = jax.random.uniform(phase_key, (BANDS,), jnp.float32) * (2.0 * math.pi)
    angles = index.astype(jnp.float32) * (2.0 * math.pi / NG) + offsets[:, None, None, None]
    shape = (BANDS, NG, NG, NG)
    heights = jax.random.uniform(height_key, (BANDS,), jnp.float32, 3.5, 4.0)
    rough = jnp.clip(jax.random.normal(rough_key, shape, jnp.float32), -6.0, 6.0) * 0.1
    return heights[:, None, None, None] * jnp.cos(angles) + rough


def setup_inputs(seed: int = 0) -> dict:
    seeds = jax.random.split(jax.random.key(seed), 2)
    orbitals = draw_orbitals(jax.random.fold_in(seeds[1], 71), 0)
    return {"orbitals": orbitals}


highest = lax.Precision.HIGHEST


def cas_table(length):
    indices = jnp.arange(length, dtype=jnp.int32)
    product = (indices[:, None] * indices[None, :]) % length
    phases = product.astype(jnp.float32) * (2.0 * math.pi / length)
    return jnp.cos(phases) + jnp.sin(phases)


def wave_square(indices, length):
    return 4.0 * jnp.sin(indices.astype(jnp.float32) * (math.pi / length)) ** 2


def reference(orbitals):
    hartley = cas_table(NG)
    waves = wave_square(jnp.arange(NG, dtype=jnp.int32), NG)
    square = waves[:, None, None] + waves[None, :, None] + waves[None, None, :]
    kernel = jnp.where(square > 0, 1.0 / jnp.where(square > 0, square, 1.0), 0.0)

    def potential(density):
        field = jnp.einsum('xk,zyx->zyk', hartley, density, precision=highest)
        field = jnp.einsum('yk,zyx->zkx', hartley, field, precision=highest)
        field = jnp.einsum('zk,zyx->kyx', hartley, field, precision=highest)
        field = field * kernel
        field = jnp.einsum('zk,zyx->kyx', hartley, field, precision=highest)
        field = jnp.einsum('xk,zyx->zyk', hartley, field, precision=highest)
        field = jnp.einsum('yk,zyx->zkx', hartley, field, precision=highest)
        return field / float(NG ** 3)

    def pair_field(members):
        return potential(members[0] * members[1])

    total = jnp.zeros(orbitals.shape, jnp.float32)
    for offset in range(1, STEPS + 1):
        visiting = jnp.roll(orbitals, offset, axis=0)
        potentials = lax.map(pair_field, (orbitals, visiting))
        total = total + potentials * visiting + jnp.roll(potentials * orbitals, -offset, axis=0)
    return total
```

```python
import functools
import math

import jax
import jax.numpy as jnp
from jax import lax
from jax.experimental import pallas as pl
from jax.experimental.pallas import tpu as pltpu
from jax.sharding import PartitionSpec as P

CHUNKS = 4

high = lax.Precision.HIGH


def passed_along(value, axis, steps):
    count = lax.axis_size(axis)
    pairs = [(source, (source + steps) % count) for source in range(count)]
    return lax.ppermute(value, axis, pairs)


def cas_table(rows, columns, length):
    product = rows[:, None] * columns[None, :] % length
    phases = product.astype(jnp.float32) * (2.0 * math.pi / length)
    return jnp.cos(phases) + jnp.sin(phases)


def wave_square(indices, length):
    return 4.0 * jnp.sin(indices.astype(jnp.float32) * (math.pi / length)) ** 2


def halves(value):
    upper = value.astype(jnp.bfloat16)
    lower = (value - upper.astype(jnp.float32)).astype(jnp.bfloat16)
    return upper, lower


def table_halves(table):
    upper = lax.reduce_precision(table, exponent_bits=8, mantissa_bits=7)
    return upper.astype(jnp.bfloat16), (table - upper).astype(jnp.bfloat16)


def product3(left, right):
    dot = functools.partial(jnp.dot, preferred_element_type=jnp.float32)
    return dot(left[0], right[0]) + (dot(left[0], right[1]) + dot(left[1], right[0]))


def plane_transform(field, along_x, along_y):
    planes, rows, columns = field.shape
    flat = field.reshape(planes * rows, columns)
    flat = product3(halves(flat), along_x)
    split = halves(flat)
    out = []
    for plane in range(planes):
        part = slice(plane * rows, (plane + 1) * rows)
        out.append(product3(along_y, (split[0][part], split[1][part])))
    return out


def forward_kernel(a_ref, b_ref, xu_ref, xl_ref, yu_ref, yl_ref, *out_refs):
    density = a_ref[...] * b_ref[...]
    out = plane_transform(density, (xu_ref[...], xl_ref[...]), (yu_ref[...], yl_ref[...]))
    width = out_refs[0].shape[1]
    for plane, value in enumerate(out):
        for group, out_ref in enumerate(out_refs):
            out_ref[plane] = value[group * width : (group + 1) * width]


def inverse_kernel(groups, adds, *refs):
    pieces, refs = refs[:groups], refs[groups:]
    xu_ref, xl_ref, yu_ref, yl_ref, a_ref, b_ref = refs[:6]
    extra, (home_ref, away_ref) = refs[6:-2], refs[-2:]
    field = jnp.concatenate([piece[...] for piece in pieces], axis=1)
    out = plane_transform(field, (xu_ref[...], xl_ref[...]), (yu_ref[...], yl_ref[...]))
    for plane, value in enumerate(out):
        home = value * b_ref[plane]
        away = value * a_ref[plane]
        if adds:
            home = home + extra[0][plane]
            away = away + extra[1][plane]
        home_ref[plane] = home
        away_ref[plane] = away


def plane_block(depth):
    return max(size for size in range(1, 6) if depth % size == 0)


def plane_cost(depth, length, arrays):
    return pl.CostEstimate(
        flops=12 * depth * length**3,
        bytes_accessed=4 * arrays * depth * length**2,
        transcendentals=0,
    )


params = pltpu.CompilerParams(vmem_limit_bytes=40 * 1024 * 1024)


def forward(resident, start, visiting, tables_x, tables_y, groups):
    depth, length, _ = visiting.shape
    width = length // groups
    block = plane_block(depth)
    first = start // block
    table = pl.BlockSpec((length, length), lambda i: (0, 0))
    return pl.pallas_call(
        forward_kernel,
        grid=(depth // block,),
        in_specs=[
            pl.BlockSpec((block, length, length), lambda i: (first + i, 0, 0)),
            pl.BlockSpec((block, length, length), lambda i: (i, 0, 0)),
        ]
        + [table] * 4,
        out_specs=[pl.BlockSpec((block, width, length), lambda i: (i, 0, 0))] * groups,
        out_shape=[jax.ShapeDtypeStruct((depth, width, length), jnp.float32)] * groups,
        cost_estimate=plane_cost(depth, length, 3),
        compiler_params=params,
        name="forward",
    )(resident, visiting, *tables_x, *tables_y)


def inverse(pieces, tables_x, tables_y, resident, start, visiting, extra=()):
    groups = len(pieces)
    depth, length, _ = visiting.shape
    width = length // groups
    block = plane_block(depth)
    first = start // block
    table = pl.BlockSpec((length, length), lambda i: (0, 0))
    whole = pl.BlockSpec((block, length, length), lambda i: (i, 0, 0))
    shape = jax.ShapeDtypeStruct((depth, length, length), jnp.float32)
    return pl.pallas_call(
        functools.partial(inverse_kernel, groups, bool(extra)),
        grid=(depth // block,),
        in_specs=[pl.BlockSpec((block, width, length), lambda i: (i, 0, 0))] * groups
        + [table] * 4
        + [pl.BlockSpec((block, length, length), lambda i: (first + i, 0, 0)), whole]
        + [whole] * len(extra),
        out_specs=[whole] * 2,
        out_shape=[shape] * 2,
        cost_estimate=plane_cost(depth, length, 5 + len(extra)),
        compiler_params=params,
        name="inverse",
    )(*pieces, *tables_x, *tables_y, resident, visiting, *extra)


def shards(orbitals):
    resident = orbitals[0]
    local, _, length = resident.shape
    groups = lax.axis_size("slab")
    me = lax.axis_index("slab")
    width = length // groups
    depth = local // CHUNKS
    starts = [chunk * depth for chunk in range(CHUNKS)]
    grid = jnp.arange(length, dtype=jnp.int32)
    turned = (me * width + grid) % length
    table_x = table_halves(cas_table(grid, grid, length))
    table_y = table_halves(cas_table(turned, grid, length))
    back_y = table_halves(cas_table(grid, turned, length))
    order = jnp.concatenate(
        [(me - j) % groups * local + jnp.arange(local, dtype=jnp.int32) for j in range(groups)]
    )
    table_z = cas_table(grid, order, length)
    waves = wave_square(grid, length)
    waves_y = wave_square(me * width + jnp.arange(width, dtype=jnp.int32), length)
    square = waves[:, None, None] + waves_y[None, :, None] + waves[None, None, :]
    kernel = jnp.where(square > 0, 1.0 / jnp.where(square > 0, square, 1.0), 0.0)
    kernel = kernel / float(length**3)

    def spread(visiting):
        sent = []
        for chunk, start in enumerate(starts):
            parts = forward(resident, start, visiting[chunk], table_x, table_y, groups)
            sent.append(
                [parts[0]] + [passed_along(parts[j], "slab", j) for j in range(1, groups)]
            )
        return [sent[chunk][j] for j in range(groups) for chunk in range(CHUNKS)]

    def filtered(parts):
        field = jnp.concatenate(parts, axis=0)
        field = jnp.einsum("kz,zyx->kyx", table_z, field, precision=high)
        field = field * kernel
        return jnp.einsum("kz,kyx->zyx", table_z, field, precision=high)

    def gathered(field, start):
        parts = []
        for j in range(groups):
            part = field[j * local + start : j * local + start + depth]
            parts.append(passed_along(part, "slab", -j) if j else part)
        return parts

    near = [passed_along(resident[s : s + depth], "band", 1) for s in starts]
    far = [passed_along(part, "band", 1) for part in near]
    near_parts = spread(near)
    far_parts = spread(far)
    far_field = filtered(far_parts)
    near_field = filtered(near_parts)
    carried = []
    for chunk, start in enumerate(starts):
        parts = gathered(far_field, start)
        home, away = inverse(parts, table_x, back_y, resident, start, far[chunk])
        carried.append((home, passed_along(away, "band", -1)))
    out = []
    for chunk, start in enumerate(starts):
        parts = gathered(near_field, start)
        home, away = inverse(
            parts, table_x, back_y, resident, start, near[chunk], carried[chunk]
        )
        out.append(home + passed_along(away, "band", -1))
    return jnp.concatenate(out, axis=0)[None]


def solution(mesh):
    in_specs = (P("band", "slab", None, None),)
    out_specs = P("band", "slab", None, None)
    return jax.shard_map(shards, mesh=mesh, in_specs=in_specs, out_specs=out_specs, check_vma=False)
```

```python
import functools
import math

import jax
import jax.numpy as jnp
from jax import lax
from jax.experimental import pallas as pl
from jax.experimental.pallas import tpu as pltpu
from jax.sharding import PartitionSpec as P

CHUNKS = 4

high = lax.Precision.HIGH


def passed_along(value, axis, steps):
    count = lax.axis_size(axis)
    pairs = [(source, (source + steps) % count) for source in range(count)]
    return lax.ppermute(value, axis, pairs)


def cas_table(rows, columns, length):
    product = rows[:, None] * columns[None, :] % length
    phases = product.astype(jnp.float32) * (2.0 * math.pi / length)
    return jnp.cos(phases) + jnp.sin(phases)


def wave_square(indices, length):
    return 4.0 * jnp.sin(indices.astype(jnp.float32) * (math.pi / length)) ** 2


def halves(value):
    upper = value.astype(jnp.bfloat16)
    lower = (value - upper.astype(jnp.float32)).astype(jnp.bfloat16)
    return upper, lower


def table_halves(table):
    upper = lax.reduce_precision(table, exponent_bits=8, mantissa_bits=7)
    return upper.astype(jnp.bfloat16), (table - upper).astype(jnp.bfloat16)


def product3(left, right):
    dot = functools.partial(jnp.dot, preferred_element_type=jnp.float32)
    return dot(left[0], right[0]) + (dot(left[0], right[1]) + dot(left[1], right[0]))


def plane_transform(field, along_x, along_y):
    planes, rows, columns = field.shape
    flat = field.reshape(planes * rows, columns)
    flat = product3(halves(flat), along_x)
    split = halves(flat)
    out = []
    for plane in range(planes):
        part = slice(plane * rows, (plane + 1) * rows)
        out.append(product3(along_y, (split[0][part], split[1][part])))
    return out


def forward_kernel(a_ref, b_ref, xu_ref, xl_ref, yu_ref, yl_ref, *out_refs):
    density = a_ref[...] * b_ref[...]
    out = plane_transform(density, (xu_ref[...], xl_ref[...]), (yu_ref[...], yl_ref[...]))
    width = out_refs[0].shape[1]
    for plane, value in enumerate(out):
        for group, out_ref in enumerate(out_refs):
            out_ref[plane] = value[group * width : (group + 1) * width]


def inverse_kernel(groups, adds, *refs):
    pieces, refs = refs[:groups], refs[groups:]
    xu_ref, xl_ref, yu_ref, yl_ref, a_ref, b_ref = refs[:6]
    extra, (home_ref, away_ref) = refs[6:-2], refs[-2:]
    field = jnp.concatenate([piece[...] for piece in pieces], axis=1)
    out = plane_transform(field, (xu_ref[...], xl_ref[...]), (yu_ref[...], yl_ref[...]))
    for plane, value in enumerate(out):
        home = value * b_ref[plane]
        away = value * a_ref[plane]
        if adds:
            home = home + extra[0][plane]
            away = away + extra[1][plane]
        home_ref[plane] = home
        away_ref[plane] = away


def plane_block(depth):
    return max(size for size in range(1, 6) if depth % size == 0)


def plane_cost(depth, length, arrays):
    return pl.CostEstimate(
        flops=12 * depth * length**3,
        bytes_accessed=4 * arrays * depth * length**2,
        transcendentals=0,
    )


params = pltpu.CompilerParams(vmem_limit_bytes=40 * 1024 * 1024)


def forward(resident, start, visiting, tables_x, tables_y, groups):
    depth, length, _ = visiting.shape
    width = length // groups
    block = plane_block(depth)
    first = start // block
    table = pl.BlockSpec((length, length), lambda i: (0, 0))
    return pl.pallas_call(
        forward_kernel,
        grid=(depth // block,),
        in_specs=[
            pl.BlockSpec((block, length, length), lambda i: (first + i, 0, 0)),
            pl.BlockSpec((block, length, length), lambda i: (i, 0, 0)),
        ]
        + [table] * 4,
        out_specs=[pl.BlockSpec((block, width, length), lambda i: (i, 0, 0))] * groups,
        out_shape=[jax.ShapeDtypeStruct((depth, width, length), jnp.float32)] * groups,
        cost_estimate=plane_cost(depth, length, 3),
        compiler_params=params,
        name="forward",
    )(resident, visiting, *tables_x, *tables_y)


def inverse(pieces, tables_x, tables_y, resident, start, visiting, extra=()):
    groups = len(pieces)
    depth, length, _ = visiting.shape
    width = length // groups
    block = plane_block(depth)
    first = start // block
    table = pl.BlockSpec((length, length), lambda i: (0, 0))
    whole = pl.BlockSpec((block, length, length), lambda i: (i, 0, 0))
    shape = jax.ShapeDtypeStruct((depth, length, length), jnp.float32)
    return pl.pallas_call(
        functools.partial(inverse_kernel, groups, bool(extra)),
        grid=(depth // block,),
        in_specs=[pl.BlockSpec((block, width, length), lambda i: (i, 0, 0))] * groups
        + [table] * 4
        + [pl.BlockSpec((block, length, length), lambda i: (first + i, 0, 0)), whole]
        + [whole] * len(extra),
        out_specs=[whole] * 2,
        out_shape=[shape] * 2,
        cost_estimate=plane_cost(depth, length, 5 + len(extra)),
        compiler_params=params,
        name="inverse",
    )(*pieces, *tables_x, *tables_y, resident, visiting, *extra)


def shards(orbitals):
    resident = orbitals[0]
    local, _, length = resident.shape
    groups = lax.axis_size("slab")
    me = lax.axis_index("slab")
    width = length // groups
    depth = local // CHUNKS
    starts = [chunk * depth for chunk in range(CHUNKS)]
    grid = jnp.arange(length, dtype=jnp.int32)
    turned = (me * width + grid) % length
    table_x = table_halves(cas_table(grid, grid, length))
    table_y = table_halves(cas_table(turned, grid, length))
    back_y = table_halves(cas_table(grid, turned, length))
    order = jnp.concatenate(
        [(me - j) % groups * local + jnp.arange(local, dtype=jnp.int32) for j in range(groups)]
    )
    table_z = cas_table(grid, order, length)
    waves = wave_square(grid, length)
    waves_y = wave_square(me * width + jnp.arange(width, dtype=jnp.int32), length)
    square = waves[:, None, None] + waves_y[None, :, None] + waves[None, None, :]
    kernel = jnp.where(square > 0, 1.0 / jnp.where(square > 0, square, 1.0), 0.0)
    kernel = kernel / float(length**3)

    def spread(visiting):
        sent = []
        for chunk, start in enumerate(starts):
            parts = forward(resident, start, visiting[chunk], table_x, table_y, groups)
            sent.append(
                [parts[0]] + [passed_along(parts[j], "slab", j) for j in range(1, groups)]
            )
        return [sent[chunk][j] for j in range(groups) for chunk in range(CHUNKS)]

    def filtered(parts):
        field = jnp.concatenate(parts, axis=0)
        field = jnp.einsum("kz,zyx->kyx", table_z, field, precision=high)
        field = field * kernel
        return jnp.einsum("kz,kyx->zyx", table_z, field, precision=high)

    arrived = []

    def gathered(field, start):
        parts = []
        for j in range(groups):
            part = field[j * local + start : j * local + start + depth]
            if j:
                if len(arrived) >= 2 * (groups - 1):
                    part, _ = lax.optimization_barrier((part, arrived[-2 * (groups - 1)]))
                part = passed_along(part, "slab", -j)
                arrived.append(part)
            parts.append(part)
        return parts

    near = [passed_along(resident[s : s + depth], "band", 1) for s in starts]
    far = [passed_along(part, "band", 1) for part in near]
    near_parts = spread(near)
    far_parts = spread(far)
    near_field = filtered(near_parts)
    far_parts[-1], near_field = lax.optimization_barrier((far_parts[-1], near_field))
    far_field = filtered(far_parts)
    carried = []
    for chunk, start in enumerate(starts):
        parts = gathered(far_field, start)
        home, away = inverse(parts, table_x, back_y, resident, start, far[chunk])
        carried.append((home, passed_along(away, "band", -1)))
    out = []
    for chunk, start in enumerate(starts):
        parts = gathered(near_field, start)
        home, away = inverse(
            parts, table_x, back_y, resident, start, near[chunk], carried[chunk]
        )
        out.append(home + passed_along(away, "band", -1))
    return jnp.concatenate(out, axis=0)[None]


def solution(mesh):
    in_specs = (P("band", "slab", None, None),)
    out_specs = P("band", "slab", None, None)
    return jax.shard_map(shards, mesh=mesh, in_specs=in_specs, out_specs=out_specs, check_vma=False)
```
